32 devices in a mesh: chan: 8 (over z, x), freq: 4 (over y, core).
Axes of the slice: x: 2, y: 2, z: 4, core: 2. Of those that a mesh axis runs over, the one named last changes fastest.
Arguments:
- traces: bfloat16 [1024, 20480], P('chan', 'freq'), may hold values from -2000 to 2000
- kept_bins: int32 [128], replicated, may hold values from 1 to 255, as said below
- round_masks: int32 [2], replicated, may hold values from 1 to 7, as said below
Outputs:
- cross_spectra: float32 [2, 128, 2, 1024, 128], P(None, 'freq', None, 'chan')
- auto_spectra: float32 [128, 2, 1024, 128], P('freq', None, 'chan')
The draws below stay inside these ranges and needn't reach their ends.
Inputs may be any that keep to these rules, and one draw needn't show every extreme that they name: `kept_bins`: 128 distinct bin numbers in increasing order; 1 and 255 are among them. `round_masks`: 2 distinct numbers; in round r channel block b is paired with block b XOR round_masks[r].
All inputs are finite; a program needn't handle non-finite values.
Results may differ from the reference program's by a relative error of at most 0.0066.
Values may be sent and summed in bfloat16 or wider, within the bound.
A program may use at most 64 MiB of HBM per device.

```python
import math
import jax
import jax.numpy as jnp
from jax import lax

NS = 512
HOP = 256
KEEP = 128
CH = 128
ROUNDS = 2
WINDOWS = 80
SAMPLES = 20480
CHANNELS = 1024
N_CHAN = 8


def draw_traces(key, part):
    subkeys = jax.random.split(key, 6)
    sample_index = jnp.arange(SAMPLES, dtype=jnp.int32)
    window_index = sample_index // HOP
    noise_field = jnp.clip(jax.random.normal(subkeys[0], (CHANNELS, SAMPLES), jnp.float32), -6.0, 6.0)
    tone_bottom = 1.0
    tone_top = 10.0
    ramp_index = jnp.arange(WINDOWS, dtype=jnp.int32).astype(jnp.float32)
    window_scale = 10.0 ** jax.random.uniform(subkeys[1], (WINDOWS,), jnp.float32)
    window_scale = window_scale * (1.0 + 2.0 * ramp_index / max(WINDOWS - 1, 1))
    per_sample = window_scale[window_index]
    channel_scale = 10.0 ** jax.random.uniform(subkeys[2], (CHANNELS, 1), jnp.float32)
    tone_bin = jax.random.randint(subkeys[3], (CHANNELS, 1), 1, NS // 2)
    tone_amp = jnp.exp(jax.random.uniform(subkeys[4], (CHANNELS, 1), jnp.float32, math.log(tone_bottom), math.log(tone_top)))
    tone_phase = jax.random.uniform(subkeys[5], (CHANNELS, WINDOWS), jnp.float32, -math.pi, math.pi)[:, window_index]
    cycle_index = tone_bin * sample_index[None, :] % NS
    tone_field = tone_amp * jnp.cos(cycle_index.astype(jnp.float32) * (2.0 * math.pi / NS) + tone_phase)
    return (channel_scale * (per_sample[None, :] * noise_field + tone_field)).astype(jnp.bfloat16)


def draw_kept_bins(key, part):
    middle = jax.random.permutation(key, NS // 2 - 3)[:KEEP - 2].astype(jnp.int32) + 2
    chosen = jnp.concatenate([jnp.array([1, NS // 2 - 1], dtype=jnp.int32), middle])
    return jnp.sort(chosen)


def draw_round_masks(key, part):
    subkeys = jax.random.split(key, 2)
    others = jax.random.permutation(subkeys[0], N_CHAN - 2)[:ROUNDS - 1].astype(jnp.int32) + 1
    round_list = jnp.concatenate([others, jnp.array([N_CHAN - 1], dtype=jnp.int32)])
    return jnp.roll(round_list, jax.random.randint(subkeys[1], (), 0, ROUNDS))


def setup_inputs(seed: int = 0) -> dict:
    arg_keys = jax.random.split(jax.random.key(seed), 4)
    traces = draw_traces(jax.random.fold_in(arg_keys[3], 71), 0)
    kept_bins = draw_kept_bins(jax.random.fold_in(arg_keys[3], 71), 0)
    round_masks = draw_round_masks(jax.random.fold_in(arg_keys[3], 71), 0)
    return {"traces": traces, "kept_bins": kept_bins, "round_masks": round_masks}


EPSILON = 1e-06

def dft_table(kept_bins):
    sample_index = jnp.arange(NS, dtype=jnp.int32)
    phase_index = kept_bins[:, None] * sample_index[None, :] % NS
    angles = phase_index.astype(jnp.float32) * jnp.float32(2.0 * math.pi / NS)
    hann_taper = 0.5 - 0.5 * jnp.cos(sample_index.astype(jnp.float32) * jnp.float32(2.0 * math.pi / NS))
    stacked = jnp.stack([hann_taper * jnp.cos(angles), -hann_taper * jnp.sin(angles)], axis=1)
    return stacked.reshape(kept_bins.shape[0] * 2, NS).astype(jnp.bfloat16)

def block_whitened(channel_block, transform):
    padded = jnp.concatenate([channel_block, jnp.zeros((CH, HOP), channel_block.dtype)], axis=1)
    padded = padded.reshape(CH, WINDOWS + 1, HOP).astype(jnp.float32)
    transform_f = transform.astype(jnp.float32)
    spectra = jnp.einsum('kn,cjn->kjc', transform_f[:, :HOP], padded[:, :-1])
    spectra = spectra + jnp.einsum('kn,cjn->kjc', transform_f[:, HOP:], padded[:, 1:])
    rounded = lax.optimization_barrier(spectra.astype(jnp.bfloat16))
    values = rounded.astype(jnp.float32).reshape(KEEP, 2, WINDOWS, CH)
    power_mean = lax.optimization_barrier(jnp.sum(values * values, axis=(1, 2))) / WINDOWS
    return (values * lax.rsqrt(power_mean + EPSILON)[:, None, None, :]).astype(jnp.bfloat16)

def correlate(left_block, right_block):
    left_f = left_block.astype(jnp.float32)
    right_f = right_block.astype(jnp.float32)
    products = jnp.einsum('kpwc,kqwd->kpqcd', left_f, right_f)
    real_part = products[:, 0, 0] + products[:, 1, 1]
    imag_part = products[:, 1, 0] - products[:, 0, 1]
    return jnp.stack([real_part, imag_part], axis=1) * (1.0 / math.sqrt(WINDOWS))

def arrange(stacked):
    return jnp.transpose(stacked, (1, 2, 0, 3, 4)).reshape(KEEP, 2, CHANNELS, CH)

def reference(traces, kept_bins, round_masks):
    transform = dft_table(kept_bins)
    blocks = traces.reshape(N_CHAN, CH, SAMPLES)
    whitened = lax.map(lambda channel_block: block_whitened(channel_block, transform), blocks)
    indices = jnp.arange(N_CHAN, dtype=jnp.int32)
    auto_terms = lax.map(lambda block_index: correlate(whitened[block_index], whitened[block_index]), indices)
    crosses = []
    for round_no in range(ROUNDS):
        round_mask = round_masks[round_no]
        paired = lax.map(lambda block_index: correlate(whitened[block_index], whitened[jnp.bitwise_xor(block_index, round_mask)]), indices)
        crosses.append(arrange(paired))
    return (jnp.stack(crosses), arrange(auto_terms))
```

```python
import functools
import math

import jax
import jax.numpy as jnp
from jax import lax
from jax.experimental import pallas as pl
from jax.experimental.pallas import tpu as pltpu
from jax.sharding import PartitionSpec as P

NS = 512
HOP = NS // 2
EPSILON = 1e-06
PARTS = 2
BINS = 4


def shifted(block, axis, distance):
    devices = range(lax.axis_size(axis))
    route = [(i - distance, i) for i in devices if i - distance in devices]
    return lax.ppermute(block, axis, route)


def moved(pieces, mask):
    route = [(i, i ^ mask) for i in range(lax.axis_size("chan"))]
    return tuple(lax.ppermute(piece, "chan", route) for piece in pieces)


def dft_table(kept_bins):
    sample_index = jnp.arange(NS, dtype=jnp.int32)
    phase_index = kept_bins[:, None] * sample_index[None, :] % NS
    angles = phase_index.astype(jnp.float32) * jnp.float32(2.0 * math.pi / NS)
    hann_taper = 0.5 - 0.5 * jnp.cos(
        sample_index.astype(jnp.float32) * jnp.float32(2.0 * math.pi / NS)
    )
    stacked = jnp.stack([hann_taper * jnp.cos(angles), -hann_taper * jnp.sin(angles)], axis=1)
    return stacked.reshape(kept_bins.shape[0] * 2, NS).astype(jnp.bfloat16)


def nt_dot(a, b):
    return lax.dot_general(a, b, (((1,), (1,)), ((), ())), preferred_element_type=jnp.float32)


def spectra_kernel(frames, traces_ref, following_ref, transform_ref, out_ref, rows):
    count = transform_ref.shape[0]
    for w in range(frames - 1):
        rows[pl.ds(w, count, stride=frames), :] = nt_dot(
            transform_ref[...], traces_ref[:, w * HOP : w * HOP + NS]
        )
    last = nt_dot(transform_ref[:, :HOP], traces_ref[:, (frames - 1) * HOP :])
    last = last + nt_dot(transform_ref[:, HOP:], following_ref[...])
    rows[pl.ds(frames - 1, count, stride=frames), :] = last
    out_ref[...] = rows[...].astype(jnp.bfloat16)


def spectra_of(traces, following, transform):
    channels, samples = traces.shape
    frames = samples // HOP
    shape = (transform.shape[0] * frames, channels)
    return pl.pallas_call(
        functools.partial(spectra_kernel, frames),
        out_shape=jax.ShapeDtypeStruct(shape, jnp.bfloat16),
        in_specs=[pl.BlockSpec(memory_space=pltpu.VMEM)] * 3,
        out_specs=pl.BlockSpec(memory_space=pltpu.VMEM),
        scratch_shapes=[pltpu.VMEM(shape, jnp.float32)],
        compiler_params=pltpu.CompilerParams(vmem_limit_bytes=32 * 2**20),
    )(traces, following, transform)


def correlate_kernel(frames, windows, order_ref, *refs):
    cross_ref, auto_ref = refs[-2:]
    span = 2 * frames
    scale = 1.0 / math.sqrt(windows)
    low_first = order_ref[0]
    blocks = [
        [ref[s].astype(jnp.float32) for ref in refs[at : at + PARTS] for s in range(ref.shape[0])]
        for at in range(0, 3 * PARTS, PARTS)
    ]
    row = lax.broadcasted_iota(jnp.int32, (span, 1), 0)
    sign = jnp.where(row < frames, 1.0, -1.0).astype(jnp.float32)
    for b in range(BINS):
        whitened = []
        for block in blocks:
            values = [part[b * span : (b + 1) * span] for part in block]
            power = sum(jnp.sum(v * v, axis=0, keepdims=True) for v in values) / windows
            gain = lax.rsqrt(power + EPSILON)
            whitened.append([v * gain for v in values])
        left = jnp.concatenate(
            [
                jnp.concatenate([v, pltpu.roll(v, frames, 0) * sign], axis=1)
                for v in whitened[0]
            ],
            axis=0,
        ).astype(jnp.bfloat16)
        right = jnp.concatenate(
            [jnp.concatenate(columns, axis=1) for columns in zip(*whitened)], axis=0
        ).astype(jnp.bfloat16)
        product = scale * lax.dot_general(
            left, right, (((0,), (0,)), ((), ())), preferred_element_type=jnp.float32
        )
        channels = product.shape[0] // 2
        for p in range(2):
            half = product[p * channels : (p + 1) * channels]
            auto_ref[b, p] = half[:, :channels]
            cross_ref[low_first, b, p] = half[:, channels : 2 * channels]
            cross_ref[1 - low_first, b, p] = half[:, 2 * channels :]


def correlate(order, own, low, high, frames, windows):
    sources, rows, channels = own[0].shape
    span = 2 * frames
    bins = rows // span
    in_spec = pl.BlockSpec((sources, BINS * span, channels), lambda i, order: (0, i, 0))
    return pl.pallas_call(
        functools.partial(correlate_kernel, frames, windows),
        grid_spec=pltpu.PrefetchScalarGridSpec(
            num_scalar_prefetch=1,
            grid=(bins // BINS,),
            in_specs=[in_spec] * (3 * PARTS),
            out_specs=[
                pl.BlockSpec((2, BINS, 2, channels, channels), lambda i, order: (0, i, 0, 0, 0)),
                pl.BlockSpec((BINS, 2, channels, channels), lambda i, order: (i, 0, 0, 0)),
            ],
        ),
        out_shape=[
            jax.ShapeDtypeStruct((2, bins, 2, channels, channels), jnp.float32),
            jax.ShapeDtypeStruct((bins, 2, channels, channels), jnp.float32),
        ],
        compiler_params=pltpu.CompilerParams(vmem_limit_bytes=40 * 2**20),
    )(order, *own, *low, *high)


def pair_exchange(low_mask, high_mask, pieces):
    blocks = lax.axis_size("chan")

    def branch(low, high, pieces):
        half = blocks // 2
        if low & half and high & half:
            if low.bit_count() <= high.bit_count():
                first = moved(pieces, low)
                return first, moved(first, low ^ high)
            first = moved(pieces, high)
            return moved(first, low ^ high), first
        return moved(pieces, low), moved(pieces, high)

    pairs = [(a, b) for a in range(1, blocks) for b in range(a + 1, blocks)]
    index = (low_mask - 1) * (blocks - 1) - low_mask * (low_mask - 1) // 2
    index = index + high_mask - low_mask - 1
    return lax.switch(index, [functools.partial(branch, a, b) for a, b in pairs], pieces)


def mask_exchange(mask, pieces):
    blocks = lax.axis_size("chan")
    branches = [lambda pieces, m=m: moved(pieces, m) for m in range(1, blocks)]
    return lax.switch(mask - 1, branches, pieces)


def body(traces, kept_bins, round_masks):
    frames = traces.shape[1] // HOP
    ranks = lax.axis_size("freq")
    following = shifted(traces[:, :HOP], "freq", -1)
    spectra = spectra_of(traces, following, dft_table(kept_bins))
    arrived = lax.all_to_all(spectra, "freq", split_axis=0, concat_axis=0, tiled=True)
    arrived = arrived.reshape(ranks, -1, arrived.shape[1])
    step = ranks // PARTS
    own = tuple(arrived[i * step : (i + 1) * step] for i in range(PARTS))
    low_mask = jnp.minimum(round_masks[0], round_masks[1])
    high_mask = jnp.maximum(round_masks[0], round_masks[1])
    if lax.axis_size("chan") <= 8:
        low, high = pair_exchange(low_mask, high_mask, own)
    else:
        low, high = mask_exchange(low_mask, own), mask_exchange(high_mask, own)
    order = (round_masks[:1] > round_masks[1:]).astype(jnp.int32)
    cross, auto = correlate(order, own, low, high, frames, frames * ranks)
    return cross, auto


def solution(mesh):
    placed = (P("chan", "freq"), P(), P())
    return jax.shard_map(
        body,
        mesh=mesh,
        in_specs=placed,
        out_specs=(P(None, "freq", None, "chan", None), P("freq", None, "chan", None)),
        check_vma=False,
    )
```

```python
import functools
import math

import jax
import jax.numpy as jnp
from jax import lax
from jax.experimental import pallas as pl
from jax.experimental.pallas import tpu as pltpu
from jax.sharding import PartitionSpec as P

NS = 512
HOP = NS // 2
EPSILON = 1e-06
CHUNKS = 4
BINS = 4


def shifted(block, axis, distance):
    devices = range(lax.axis_size(axis))
    route = [(i - distance, i) for i in devices if i - distance in devices]
    return lax.ppermute(block, axis, route)


def moved(piece, mask):
    route = [(i, i ^ mask) for i in range(lax.axis_size("chan"))]
    return lax.ppermute(piece, "chan", route)


def gathered(piece):
    ranks = lax.axis_size("freq")
    piece = lax.all_to_all(piece, "freq", split_axis=0, concat_axis=0, tiled=True)
    return piece.reshape(ranks, -1, piece.shape[1])


def dft_table(kept_bins):
    sample_index = jnp.arange(NS, dtype=jnp.int32)
    phase_index = kept_bins[:, None] * sample_index[None, :] % NS
    angles = phase_index.astype(jnp.float32) * jnp.float32(2.0 * math.pi / NS)
    hann_taper = 0.5 - 0.5 * jnp.cos(
        sample_index.astype(jnp.float32) * jnp.float32(2.0 * math.pi / NS)
    )
    stacked = jnp.stack([hann_taper * jnp.cos(angles), -hann_taper * jnp.sin(angles)], axis=1)
    return stacked.reshape(kept_bins.shape[0] * 2, NS).astype(jnp.bfloat16)


def nt_dot(a, b):
    return lax.dot_general(a, b, (((1,), (1,)), ((), ())), preferred_element_type=jnp.float32)


def spectra_kernel(frames, ranks, traces_ref, following_ref, transform_ref, *refs):
    *out_refs, rows = refs
    count = transform_ref.shape[0]
    for w in range(frames - 1):
        rows[pl.ds(w, count, stride=frames), :] = nt_dot(
            transform_ref[...], traces_ref[:, w * HOP : w * HOP + NS]
        )
    last = nt_dot(transform_ref[:, :HOP], traces_ref[:, (frames - 1) * HOP :])
    last = last + nt_dot(transform_ref[:, HOP:], following_ref[...])
    rows[pl.ds(frames - 1, count, stride=frames), :] = last
    length = rows.shape[0] // (ranks * len(out_refs))
    for c, out_ref in enumerate(out_refs):
        for r in range(ranks):
            start = (r * len(out_refs) + c) * length
            out_ref[r * length : (r + 1) * length] = rows[start : start + length].astype(
                jnp.bfloat16
            )


def spectra_of(traces, following, transform, chunks):
    channels, samples = traces.shape
    frames = samples // HOP
    total = transform.shape[0] * frames
    return pl.pallas_call(
        functools.partial(spectra_kernel, frames, lax.axis_size("freq")),
        out_shape=[jax.ShapeDtypeStruct((total // chunks, channels), jnp.bfloat16)] * chunks,
        in_specs=[pl.BlockSpec(memory_space=pltpu.VMEM)] * 3,
        out_specs=[pl.BlockSpec(memory_space=pltpu.VMEM)] * chunks,
        scratch_shapes=[pltpu.VMEM((total, channels), jnp.float32)],
        compiler_params=pltpu.CompilerParams(vmem_limit_bytes=32 * 2**20),
    )(traces, following, transform)


def correlate_kernel(frames, windows, order_ref, *refs):
    cross_ref, auto_ref = refs[-2:]
    span = 2 * frames
    scale = 1.0 / math.sqrt(windows)
    low_first = order_ref[0]
    blocks = [[ref[s].astype(jnp.float32) for s in range(ref.shape[0])] for ref in refs[:3]]
    row = lax.broadcasted_iota(jnp.int32, (span, 1), 0)
    sign = jnp.where(row < frames, 1.0, -1.0).astype(jnp.float32)
    for b in range(BINS):
        whitened = []
        for block in blocks:
            values = [part[b * span : (b + 1) * span] for part in block]
            power = sum(jnp.sum(v * v, axis=0, keepdims=True) for v in values) / windows
            gain = lax.rsqrt(power + EPSILON)
            whitened.append([v * gain for v in values])
        left = jnp.concatenate(
            [
                jnp.concatenate([v, pltpu.roll(v, frames, 0) * sign], axis=1)
                for v in whitened[0]
            ],
            axis=0,
        ).astype(jnp.bfloat16)
        right = jnp.concatenate(
            [jnp.concatenate(columns, axis=1) for columns in zip(*whitened)], axis=0
        ).astype(jnp.bfloat16)
        product = scale * lax.dot_general(
            left, right, (((0,), (0,)), ((), ())), preferred_element_type=jnp.float32
        )
        channels = product.shape[0] // 2
        for p in range(2):
            half = product[p * channels : (p + 1) * channels]
            auto_ref[b, p] = half[:, :channels]
            cross_ref[low_first, b, p] = half[:, channels : 2 * channels]
            cross_ref[1 - low_first, b, p] = half[:, 2 * channels :]


def correlate(order, blocks, results, chunk, chunks, frames, windows):
    sources, rows, channels = blocks[0].shape
    bins = rows // (2 * frames)
    first = chunk * bins // BINS
    in_spec = pl.BlockSpec((sources, BINS * 2 * frames, channels), lambda i, order: (0, i, 0))
    shapes = [
        (2, bins * chunks, 2, channels, channels),
        (bins * chunks, 2, channels, channels),
    ]
    return pl.pallas_call(
        functools.partial(correlate_kernel, frames, windows),
        grid_spec=pltpu.PrefetchScalarGridSpec(
            num_scalar_prefetch=1,
            grid=(bins // BINS,),
            in_specs=[in_spec] * 3 + [pl.BlockSpec(memory_space=pl.ANY)] * len(results),
            out_specs=[
                pl.BlockSpec(
                    (2, BINS, 2, channels, channels), lambda i, order: (0, first + i, 0, 0, 0)
                ),
                pl.BlockSpec((BINS, 2, channels, channels), lambda i, order: (first + i, 0, 0, 0)),
            ],
        ),
        out_shape=[jax.ShapeDtypeStruct(shape, jnp.float32) for shape in shapes],
        input_output_aliases={4 + i: i for i in range(len(results))},
        cost_estimate=pl.CostEstimate(
            flops=2 * bins * sources * 2 * frames * 6 * channels * channels,
            bytes_accessed=6 * sources * rows * channels + 24 * bins * channels * channels,
            transcendentals=0,
        ),
        compiler_params=pltpu.CompilerParams(vmem_limit_bytes=40 * 2**20),
    )(order, *blocks, *results)


def branch(low, high, frames, windows, order, opening, spectra):
    half = lax.axis_size("chan") // 2
    chunks = len(spectra) + 1
    own = [opening] + [gathered(piece) for piece in spectra]
    relayed = bool(low & half and high & half)
    lead = low if relayed and low.bit_count() <= high.bit_count() else high
    trail = low ^ high ^ lead
    results, before = (), None
    for c in range(chunks):
        block = own[c]
        if before is not None:
            block, before = lax.optimization_barrier((block, before))
        leading = moved(block, lead)
        trailing = moved(leading, low ^ high) if relayed else moved(block, trail)
        before = leading
        pair = (leading, trailing) if lead == low else (trailing, leading)
        results = correlate(order, (own[c], *pair), results, c, chunks, frames, windows)
    return tuple(results)


def mask_exchange(mask, piece):
    blocks = lax.axis_size("chan")
    branches = [functools.partial(moved, mask=m) for m in range(1, blocks)]
    return lax.switch(mask - 1, branches, piece)


def body(traces, kept_bins, round_masks):
    frames = traces.shape[1] // HOP
    blocks = lax.axis_size("chan")
    ranks = lax.axis_size("freq")
    windows = frames * ranks
    chunks = min(CHUNKS, kept_bins.shape[0] // ranks // BINS)
    following = shifted(traces[:, :HOP], "freq", -1)
    spectra = spectra_of(traces, following, dft_table(kept_bins), chunks)
    low_mask = jnp.minimum(round_masks[0], round_masks[1])
    high_mask = jnp.maximum(round_masks[0], round_masks[1])
    order = (round_masks[:1] > round_masks[1:]).astype(jnp.int32)
    if blocks <= 8:
        pairs = [(a, b) for a in range(1, blocks) for b in range(a + 1, blocks)]
        index = (low_mask - 1) * (blocks - 1) - low_mask * (low_mask - 1) // 2
        index = index + high_mask - low_mask - 1
        branches = [functools.partial(branch, a, b, frames, windows) for a, b in pairs]
        return lax.switch(index, branches, order, gathered(spectra[0]), tuple(spectra[1:]))
    results = ()
    for c in range(chunks):
        own = gathered(spectra[c])
        three = (own, mask_exchange(low_mask, own), mask_exchange(high_mask, own))
        results = correlate(order, three, results, c, chunks, frames, windows)
    return tuple(results)


def solution(mesh):
    placed = (P("chan", "freq"), P(), P())
    return jax.shard_map(
        body,
        mesh=mesh,
        in_specs=placed,
        out_specs=(P(None, "freq", None, "chan", None), P("freq", None, "chan", None)),
        check_vma=False,
    )
```

```python
import functools
import math

import jax
import jax.numpy as jnp
from jax import lax
from jax.experimental import pallas as pl
from jax.experimental.pallas import tpu as pltpu
from jax.sharding import PartitionSpec as P

NS = 512
HOP = NS // 2
EPSILON = 1e-06
PARTS = 2
BINS = 4


def shifted(block, axis, distance):
    devices = range(lax.axis_size(axis))
    route = [(i - distance, i) for i in devices if i - distance in devices]
    return lax.ppermute(block, axis, route)


def moved(piece, mask):
    route = [(i, i ^ mask) for i in range(lax.axis_size("chan"))]
    return lax.ppermute(piece, "chan", route)


def dft_table(kept_bins):
    sample_index = jnp.arange(NS, dtype=jnp.int32)
    phase_index = kept_bins[:, None] * sample_index[None, :] % NS
    angles = phase_index.astype(jnp.float32) * jnp.float32(2.0 * math.pi / NS)
    hann_taper = 0.5 - 0.5 * jnp.cos(
        sample_index.astype(jnp.float32) * jnp.float32(2.0 * math.pi / NS)
    )
    stacked = jnp.stack([hann_taper * jnp.cos(angles), -hann_taper * jnp.sin(angles)], axis=1)
    return stacked.reshape(kept_bins.shape[0] * 2, NS).astype(jnp.bfloat16)


def nt_dot(a, b):
    return lax.dot_general(a, b, (((1,), (1,)), ((), ())), preferred_element_type=jnp.float32)


def spectra_kernel(frames, ranks, *refs):
    traces_ref, following_ref, transform_ref, arrived_ref = refs[:4]
    rows, sends, send_sem, recv_sem, own_sem = refs[4:]
    me = lax.axis_index("freq")
    peers = [lax.rem(me + d, ranks) for d in range(1, ranks)]
    barrier = pltpu.get_barrier_semaphore()
    for peer in peers:
        pl.semaphore_signal(
            barrier, inc=1, device_id={"freq": peer}, device_id_type=pl.DeviceIdType.MESH
        )
    count = transform_ref.shape[0]
    for w in range(frames - 1):
        rows[pl.ds(w, count, stride=frames), :] = nt_dot(
            transform_ref[...], traces_ref[:, w * HOP : w * HOP + NS]
        )
    last = nt_dot(transform_ref[:, :HOP], traces_ref[:, (frames - 1) * HOP :])
    last = last + nt_dot(transform_ref[:, HOP:], following_ref[...])
    rows[pl.ds(frames - 1, count, stride=frames), :] = last
    length = sends.shape[1]
    for r in range(ranks):
        sends[r] = rows[r * length : (r + 1) * length].astype(jnp.bfloat16)
    pl.semaphore_wait(barrier, ranks - 1)
    copies = [
        pltpu.make_async_remote_copy(
            src_ref=sends.at[peer],
            dst_ref=arrived_ref.at[me],
            send_sem=send_sem.at[i],
            recv_sem=recv_sem.at[i],
            device_id={"freq": peer},
            device_id_type=pl.DeviceIdType.MESH,
        )
        for i, peer in enumerate(peers)
    ]
    copies.append(pltpu.make_async_copy(sends.at[me], arrived_ref.at[me], own_sem))
    for copy in copies:
        copy.start()
    for copy in copies:
        copy.wait()


def spectra_of(traces, following, transform):
    channels, samples = traces.shape
    frames = samples // HOP
    ranks = lax.axis_size("freq")
    total = transform.shape[0] * frames
    shape = (ranks, total // ranks, channels)
    return pl.pallas_call(
        functools.partial(spectra_kernel, frames, ranks),
        out_shape=jax.ShapeDtypeStruct(shape, jnp.bfloat16),
        in_specs=[pl.BlockSpec(memory_space=pltpu.VMEM)] * 3,
        out_specs=pl.BlockSpec(memory_space=pl.ANY),
        scratch_shapes=[
            pltpu.VMEM((total, channels), jnp.float32),
            pltpu.VMEM(shape, jnp.bfloat16),
            pltpu.SemaphoreType.DMA((ranks - 1,)),
            pltpu.SemaphoreType.DMA((ranks - 1,)),
            pltpu.SemaphoreType.DMA,
        ],
        compiler_params=pltpu.CompilerParams(
            collective_id=0, has_side_effects=True, vmem_limit_bytes=32 * 2**20
        ),
    )(traces, following, transform)


def correlate_kernel(frames, windows, order_ref, *refs):
    cross_ref, auto_ref = refs[-2:]
    span = 2 * frames
    scale = 1.0 / math.sqrt(windows)
    low_first = order_ref[0]
    blocks = [
        [ref[s].astype(jnp.float32) for ref in refs[at : at + PARTS] for s in range(ref.shape[0])]
        for at in range(0, 3 * PARTS, PARTS)
    ]
    row = lax.broadcasted_iota(jnp.int32, (span, 1), 0)
    sign = jnp.where(row < frames, 1.0, -1.0).astype(jnp.float32)
    for b in range(BINS):
        whitened = []
        for block in blocks:
            values = [part[b * span : (b + 1) * span] for part in block]
            power = sum(jnp.sum(v * v, axis=0, keepdims=True) for v in values) / windows
            gain = lax.rsqrt(power + EPSILON)
            whitened.append([v * gain for v in values])
        left = jnp.concatenate(
            [
                jnp.concatenate([v, pltpu.roll(v, frames, 0) * sign], axis=1)
                for v in whitened[0]
            ],
            axis=0,
        ).astype(jnp.bfloat16)
        right = jnp.concatenate(
            [jnp.concatenate(columns, axis=1) for columns in zip(*whitened)], axis=0
        ).astype(jnp.bfloat16)
        product = scale * lax.dot_general(
            left, right, (((0,), (0,)), ((), ())), preferred_element_type=jnp.float32
        )
        channels = product.shape[0] // 2
        for p in range(2):
            half = product[p * channels : (p + 1) * channels]
            auto_ref[b, p] = half[:, :channels]
            cross_ref[low_first, b, p] = half[:, channels : 2 * channels]
            cross_ref[1 - low_first, b, p] = half[:, 2 * channels :]


def correlate(order, own, low, high, frames, windows):
    sources, rows, channels = own[0].shape
    span = 2 * frames
    bins = rows // span
    in_spec = pl.BlockSpec((sources, BINS * span, channels), lambda i, order: (0, i, 0))
    return pl.pallas_call(
        functools.partial(correlate_kernel, frames, windows),
        grid_spec=pltpu.PrefetchScalarGridSpec(
            num_scalar_prefetch=1,
            grid=(bins // BINS,),
            in_specs=[in_spec] * (3 * PARTS),
            out_specs=[
                pl.BlockSpec((2, BINS, 2, channels, channels), lambda i, order: (0, i, 0, 0, 0)),
                pl.BlockSpec((BINS, 2, channels, channels), lambda i, order: (i, 0, 0, 0)),
            ],
        ),
        out_shape=[
            jax.ShapeDtypeStruct((2, bins, 2, channels, channels), jnp.float32),
            jax.ShapeDtypeStruct((bins, 2, channels, channels), jnp.float32),
        ],
        compiler_params=pltpu.CompilerParams(vmem_limit_bytes=40 * 2**20),
    )(order, *own, *low, *high)


def pair_exchange(low_mask, high_mask, pieces):
    blocks = lax.axis_size("chan")

    def branch(low, high, pieces):
        half = blocks // 2
        if not (low & half and high & half):
            return tuple([moved(piece, mask) for piece in pieces] for mask in (low, high))
        lead = low if low.bit_count() <= high.bit_count() else high
        leading, trailing = [], []
        for piece in pieces:
            if leading:
                piece, leading[-1] = lax.optimization_barrier((piece, leading[-1]))
            leading.append(moved(piece, lead))
            trailing.append(moved(leading[-1], low ^ high))
        return (leading, trailing) if lead == low else (trailing, leading)

    pairs = [(a, b) for a in range(1, blocks) for b in range(a + 1, blocks)]
    index = (low_mask - 1) * (blocks - 1) - low_mask * (low_mask - 1) // 2
    index = index + high_mask - low_mask - 1
    return lax.switch(index, [functools.partial(branch, a, b) for a, b in pairs], pieces)


def mask_exchange(mask, pieces):
    blocks = lax.axis_size("chan")
    branches = [
        lambda pieces, m=m: [moved(piece, m) for piece in pieces] for m in range(1, blocks)
    ]
    return lax.switch(mask - 1, branches, pieces)


def body(traces, kept_bins, round_masks):
    frames = traces.shape[1] // HOP
    ranks = lax.axis_size("freq")
    following = shifted(traces[:, :HOP], "freq", -1)
    arrived = spectra_of(traces, following, dft_table(kept_bins))
    step = ranks // PARTS
    own = tuple(arrived[i * step : (i + 1) * step] for i in range(PARTS))
    low_mask = jnp.minimum(round_masks[0], round_masks[1])
    high_mask = jnp.maximum(round_masks[0], round_masks[1])
    if lax.axis_size("chan") <= 8:
        low, high = pair_exchange(low_mask, high_mask, own)
    else:
        low, high = mask_exchange(low_mask, own), mask_exchange(high_mask, own)
    order = (round_masks[:1] > round_masks[1:]).astype(jnp.int32)
    cross, auto = correlate(order, own, low, high, frames, frames * ranks)
    return cross, auto


def solution(mesh):
    placed = (P("chan", "freq"), P(), P())
    return jax.shard_map(
        body,
        mesh=mesh,
        in_specs=placed,
        out_specs=(P(None, "freq", None, "chan", None), P("freq", None, "chan", None)),
        check_vma=False,
    )
```

```python
import functools
import math

import jax
import jax.numpy as jnp
from jax import lax
from jax.experimental import pallas as pl
from jax.experimental.pallas import tpu as pltpu
from jax.sharding import PartitionSpec as P

NS = 512
HOP = NS // 2
EPSILON = 1e-06
PARTS = 4
BINS = 4


def moved(piece, mask):
    route = [(i, i ^ mask) for i in range(lax.axis_size("chan"))]
    return lax.ppermute(piece, "chan", route)


def dft_table(kept_bins):
    sample_index = jnp.arange(NS, dtype=jnp.int32)
    phase_index = kept_bins[:, None] * sample_index[None, :] % NS
    angles = phase_index.astype(jnp.float32) * jnp.float32(2.0 * math.pi / NS)
    hann_taper = 0.5 - 0.5 * jnp.cos(
        sample_index.astype(jnp.float32) * jnp.float32(2.0 * math.pi / NS)
    )
    stacked = jnp.stack([hann_taper * jnp.cos(angles), -hann_taper * jnp.sin(angles)], axis=1)
    return stacked.reshape(kept_bins.shape[0] * 2, NS).astype(jnp.bfloat16)


def nt_dot(a, b):
    return lax.dot_general(a, b, (((1,), (1,)), ((), ())), preferred_element_type=jnp.float32)


def spectra_kernel(frames, ranks, *refs):
    traces_ref, transform_ref, arrived_ref = refs[:3]
    rows, sends, following_ref, send_sem, recv_sem, own_sem, edge_sem = refs[3:]
    me = lax.axis_index("freq")
    peers = [lax.rem(me + d, ranks) for d in range(1, ranks)]
    barrier = pltpu.get_barrier_semaphore()
    for peer in peers:
        pl.semaphore_signal(
            barrier, inc=1, device_id={"freq": peer}, device_id_type=pl.DeviceIdType.MESH
        )
    edge = pltpu.make_async_remote_copy(
        src_ref=traces_ref.at[:, pl.ds(0, HOP)],
        dst_ref=following_ref,
        send_sem=edge_sem.at[0],
        recv_sem=edge_sem.at[1],
        device_id={"freq": lax.rem(me + ranks - 1, ranks)},
        device_id_type=pl.DeviceIdType.MESH,
    )
    count = transform_ref.shape[0]
    for w in range(frames - 1):
        if w == frames // 2:
            pl.semaphore_wait(barrier, ranks - 1)
            edge.start()
        rows[pl.ds(w, count, stride=frames), :] = nt_dot(
            transform_ref[...], traces_ref[:, w * HOP : w * HOP + NS]
        )
    last = nt_dot(transform_ref[:, :HOP], traces_ref[:, (frames - 1) * HOP :])
    edge.wait()
    beyond = nt_dot(transform_ref[:, HOP:], following_ref[...])
    last = last + jnp.where(me < ranks - 1, beyond, 0.0)
    rows[pl.ds(frames - 1, count, stride=frames), :] = last
    length = sends.shape[1]
    for r in range(ranks):
        sends[r] = rows[r * length : (r + 1) * length].astype(jnp.bfloat16)
    copies = [
        pltpu.make_async_remote_copy(
            src_ref=sends.at[peer],
            dst_ref=arrived_ref.at[me],
            send_sem=send_sem.at[i],
            recv_sem=recv_sem.at[i],
            device_id={"freq": peer},
            device_id_type=pl.DeviceIdType.MESH,
        )
        for i, peer in enumerate(peers)
    ]
    copies.append(pltpu.make_async_copy(sends.at[me], arrived_ref.at[me], own_sem))
    for copy in copies:
        copy.start()
    for copy in copies:
        copy.wait()


def spectra_of(traces, transform):
    channels, samples = traces.shape
    frames = samples // HOP
    ranks = lax.axis_size("freq")
    total = transform.shape[0] * frames
    shape = (ranks, total // ranks, channels)
    return pl.pallas_call(
        functools.partial(spectra_kernel, frames, ranks),
        out_shape=jax.ShapeDtypeStruct(shape, jnp.bfloat16),
        in_specs=[pl.BlockSpec(memory_space=pltpu.VMEM)] * 2,
        out_specs=pl.BlockSpec(memory_space=pl.ANY),
        scratch_shapes=[
            pltpu.VMEM((total, channels), jnp.float32),
            pltpu.VMEM(shape, jnp.bfloat16),
            pltpu.VMEM((channels, HOP), jnp.bfloat16),
            pltpu.SemaphoreType.DMA((ranks - 1,)),
            pltpu.SemaphoreType.DMA((ranks - 1,)),
            pltpu.SemaphoreType.DMA,
            pltpu.SemaphoreType.DMA((2,)),
        ],
        compiler_params=pltpu.CompilerParams(
            collective_id=0, has_side_effects=True, vmem_limit_bytes=32 * 2**20
        ),
    )(traces, transform)


def correlate_kernel(frames, windows, masks_ref, *refs):
    cross_ref, auto_ref = refs[-2:]
    span = 2 * frames
    scale = 1.0 / math.sqrt(windows)
    low_first = jnp.where(masks_ref[0] > masks_ref[1], 1, 0)
    blocks = [
        [ref[s].astype(jnp.float32) for ref in refs[at : at + PARTS] for s in range(ref.shape[0])]
        for at in range(0, 3 * PARTS, PARTS)
    ]
    row = lax.broadcasted_iota(jnp.int32, (span, 1), 0)
    sign = jnp.where(row < frames, 1.0, -1.0).astype(jnp.float32)
    for b in range(BINS):
        whitened = []
        for block in blocks:
            values = [part[b * span : (b + 1) * span] for part in block]
            power = sum(jnp.sum(v * v, axis=0, keepdims=True) for v in values) / windows
            gain = lax.rsqrt(power + EPSILON)
            whitened.append([v * gain for v in values])
        left = jnp.concatenate(
            [
                jnp.concatenate([v, pltpu.roll(v, frames, 0) * sign], axis=1)
                for v in whitened[0]
            ],
            axis=0,
        ).astype(jnp.bfloat16)
        right = jnp.concatenate(
            [jnp.concatenate(columns, axis=1) for columns in zip(*whitened)], axis=0
        ).astype(jnp.bfloat16)
        product = scale * lax.dot_general(
            left, right, (((0,), (0,)), ((), ())), preferred_element_type=jnp.float32
        )
        channels = product.shape[0] // 2
        for p in range(2):
            half = product[p * channels : (p + 1) * channels]
            auto_ref[b, p] = half[:, :channels]
            cross_ref[low_first, b, p] = half[:, channels : 2 * channels]
            cross_ref[1 - low_first, b, p] = half[:, 2 * channels :]


def correlate(masks, own, low, high, frames, windows):
    sources, rows, channels = own[0].shape
    span = 2 * frames
    bins = rows // span
    in_spec = pl.BlockSpec((sources, BINS * span, channels), lambda i, masks: (0, i, 0))
    return pl.pallas_call(
        functools.partial(correlate_kernel, frames, windows),
        grid_spec=pltpu.PrefetchScalarGridSpec(
            num_scalar_prefetch=1,
            grid=(bins // BINS,),
            in_specs=[in_spec] * (3 * PARTS),
            out_specs=[
                pl.BlockSpec((2, BINS, 2, channels, channels), lambda i, masks: (0, i, 0, 0, 0)),
                pl.BlockSpec((BINS, 2, channels, channels), lambda i, masks: (i, 0, 0, 0)),
            ],
        ),
        out_shape=[
            jax.ShapeDtypeStruct((2, bins, 2, channels, channels), jnp.float32),
            jax.ShapeDtypeStruct((bins, 2, channels, channels), jnp.float32),
        ],
        compiler_params=pltpu.CompilerParams(vmem_limit_bytes=40 * 2**20),
    )(masks, *own, *low, *high)


def pair_exchange(masks, pieces):
    blocks = lax.axis_size("chan")

    def branch(low, high, pieces):
        half = blocks // 2
        if not (low & half and high & half):
            return tuple([moved(piece, mask) for piece in pieces] for mask in (low, high))
        lead = low if low.bit_count() <= high.bit_count() else high
        leading, trailing = [], []
        for piece in pieces:
            if leading:
                piece, leading[-1] = lax.optimization_barrier((piece, leading[-1]))
            leading.append(moved(piece, lead))
            trailing.append(moved(leading[-1], low ^ high))
        return (leading, trailing) if lead == low else (trailing, leading)

    pairs = [(a, b) for a in range(1, blocks) for b in range(a + 1, blocks)]
    table = [0] * (blocks * blocks)
    for i, (a, b) in enumerate(pairs):
        table[a * blocks + b] = table[b * blocks + a] = i
    place = masks[:1] * blocks + masks[1:]
    index = lax.dynamic_index_in_dim(jnp.array(table, jnp.int32), place[0], keepdims=False)
    return lax.switch(index, [functools.partial(branch, a, b) for a, b in pairs], pieces)


def mask_exchange(mask, pieces):
    blocks = lax.axis_size("chan")
    branches = [
        lambda pieces, m=m: [moved(piece, m) for piece in pieces] for m in range(1, blocks)
    ]
    return lax.switch(mask - 1, branches, pieces)


def body(traces, kept_bins, round_masks):
    frames = traces.shape[1] // HOP
    ranks = lax.axis_size("freq")
    arrived = spectra_of(traces, dft_table(kept_bins))
    step = ranks // PARTS
    own = tuple(arrived[i * step : (i + 1) * step] for i in range(PARTS))
    if lax.axis_size("chan") <= 8:
        low, high = pair_exchange(round_masks, own)
    else:
        low = mask_exchange(jnp.minimum(round_masks[0], round_masks[1]), own)
        high = mask_exchange(jnp.maximum(round_masks[0], round_masks[1]), own)
    cross, auto = correlate(round_masks, own, low, high, frames, frames * ranks)
    return cross, auto


def solution(mesh):
    placed = (P("chan", "freq"), P(), P())
    return jax.shard_map(
        body,
        mesh=mesh,
        in_specs=placed,
        out_specs=(P(None, "freq", None, "chan", None), P("freq", None, "chan", None)),
        check_vma=False,
    )
```

```python
import functools
import math

import jax
import jax.numpy as jnp
from jax import lax
from jax.experimental import pallas as pl
from jax.experimental.pallas import tpu as pltpu
from jax.sharding import PartitionSpec as P

NS = 512
HOP = NS // 2
EPSILON = 1e-06
PARTS = 2
BINS = 4


def moved(piece, mask):
    route = [(i, i ^ mask) for i in range(lax.axis_size("chan"))]
    return lax.ppermute(piece, "chan", route)


def dft_table(kept_bins):
    sample_index = jnp.arange(NS, dtype=jnp.int32)
    phase_index = kept_bins[:, None] * sample_index[None, :] % NS
    angles = phase_index.astype(jnp.float32) * jnp.float32(2.0 * math.pi / NS)
    hann_taper = 0.5 - 0.5 * jnp.cos(
        sample_index.astype(jnp.float32) * jnp.float32(2.0 * math.pi / NS)
    )
    stacked = jnp.stack([hann_taper * jnp.cos(angles), -hann_taper * jnp.sin(angles)], axis=1)
    return stacked.reshape(kept_bins.shape[0] * 2, NS).astype(jnp.bfloat16)


def nt_dot(a, b):
    return lax.dot_general(a, b, (((1,), (1,)), ((), ())), preferred_element_type=jnp.float32)


def spectra_kernel(frames, ranks, *refs):
    masks_ref, traces_ref, transform_ref, arrived_ref, index_ref = refs[:5]
    rows, sends, following_ref, send_sem, recv_sem, own_sem, edge_sem = refs[5:]
    me = lax.axis_index("freq")
    peers = [lax.rem(me + d, ranks) for d in range(1, ranks)]
    barrier = pltpu.get_barrier_semaphore()
    for peer in peers:
        pl.semaphore_signal(
            barrier, inc=1, device_id={"freq": peer}, device_id_type=pl.DeviceIdType.MESH
        )
    low = jnp.minimum(masks_ref[0], masks_ref[1])
    high = jnp.maximum(masks_ref[0], masks_ref[1])
    before = (low - 1) * (lax.axis_size("chan") - 1) - lax.div(low * (low - 1), 2)
    index_ref[0] = before + high - low - 1
    edge = pltpu.make_async_remote_copy(
        src_ref=traces_ref.at[:, pl.ds(0, HOP)],
        dst_ref=following_ref,
        send_sem=edge_sem.at[0],
        recv_sem=edge_sem.at[1],
        device_id={"freq": lax.rem(me + ranks - 1, ranks)},
        device_id_type=pl.DeviceIdType.MESH,
    )
    count = transform_ref.shape[0]
    for w in range(frames - 1):
        if w == frames // 2:
            pl.semaphore_wait(barrier, ranks - 1)
            edge.start()
        rows[pl.ds(w, count, stride=frames), :] = nt_dot(
            transform_ref[...], traces_ref[:, w * HOP : w * HOP + NS]
        )
    last = nt_dot(transform_ref[:, :HOP], traces_ref[:, (frames - 1) * HOP :])
    edge.wait()
    beyond = nt_dot(transform_ref[:, HOP:], following_ref[...])
    last = last + jnp.where(me < ranks - 1, beyond, 0.0)
    rows[pl.ds(frames - 1, count, stride=frames), :] = last
    length = sends.shape[1]
    for r in range(ranks):
        sends[r] = rows[r * length : (r + 1) * length].astype(jnp.bfloat16)
    copies = [
        pltpu.make_async_remote_copy(
            src_ref=sends.at[peer],
            dst_ref=arrived_ref.at[me],
            send_sem=send_sem.at[i],
            recv_sem=recv_sem.at[i],
            device_id={"freq": peer},
            device_id_type=pl.DeviceIdType.MESH,
        )
        for i, peer in enumerate(peers)
    ]
    copies.append(pltpu.make_async_copy(sends.at[me], arrived_ref.at[me], own_sem))
    for copy in copies:
        copy.start()
    for copy in copies:
        copy.wait()


def spectra_of(masks, traces, transform):
    channels, samples = traces.shape
    frames = samples // HOP
    ranks = lax.axis_size("freq")
    total = transform.shape[0] * frames
    shape = (ranks, total // ranks, channels)
    return pl.pallas_call(
        functools.partial(spectra_kernel, frames, ranks),
        out_shape=[
            jax.ShapeDtypeStruct(shape, jnp.bfloat16),
            jax.ShapeDtypeStruct((1,), jnp.int32),
        ],
        in_specs=[
            pl.BlockSpec(memory_space=pltpu.SMEM),
            pl.BlockSpec(memory_space=pltpu.VMEM),
            pl.BlockSpec(memory_space=pltpu.VMEM),
        ],
        out_specs=[
            pl.BlockSpec(memory_space=pl.ANY),
            pl.BlockSpec(memory_space=pltpu.SMEM),
        ],
        scratch_shapes=[
            pltpu.VMEM((total, channels), jnp.float32),
            pltpu.VMEM(shape, jnp.bfloat16),
            pltpu.VMEM((channels, HOP), jnp.bfloat16),
            pltpu.SemaphoreType.DMA((ranks - 1,)),
            pltpu.SemaphoreType.DMA((ranks - 1,)),
            pltpu.SemaphoreType.DMA,
            pltpu.SemaphoreType.DMA((2,)),
        ],
        compiler_params=pltpu.CompilerParams(
            collective_id=0, has_side_effects=True, vmem_limit_bytes=32 * 2**20
        ),
    )(masks, traces, transform)


def correlate_kernel(frames, windows, masks_ref, *refs):
    cross_ref, auto_ref = refs[-2:]
    span = 2 * frames
    scale = 1.0 / math.sqrt(windows)
    low_first = jnp.where(masks_ref[0] > masks_ref[1], 1, 0)
    blocks = [
        [ref[s].astype(jnp.float32) for ref in refs[at : at + PARTS] for s in range(ref.shape[0])]
        for at in range(0, 3 * PARTS, PARTS)
    ]
    row = lax.broadcasted_iota(jnp.int32, (span, 1), 0)
    sign = jnp.where(row < frames, 1.0, -1.0).astype(jnp.float32)
    for b in range(BINS):
        whitened = []
        for block in blocks:
            values = [part[b * span : (b + 1) * span] for part in block]
            power = sum(jnp.sum(v * v, axis=0, keepdims=True) for v in values) / windows
            gain = lax.rsqrt(power + EPSILON)
            whitened.append([v * gain for v in values])
        left = jnp.concatenate(
            [
                jnp.concatenate([v, pltpu.roll(v, frames, 0) * sign], axis=1)
                for v in whitened[0]
            ],
            axis=0,
        ).astype(jnp.bfloat16)
        right = jnp.concatenate(
            [jnp.concatenate(columns, axis=1) for columns in zip(*whitened)], axis=0
        ).astype(jnp.bfloat16)
        product = scale * lax.dot_general(
            left, right, (((0,), (0,)), ((), ())), preferred_element_type=jnp.float32
        )
        channels = product.shape[0] // 2
        for p in range(2):
            half = product[p * channels : (p + 1) * channels]
            auto_ref[b, p] = half[:, :channels]
            cross_ref[low_first, b, p] = half[:, channels : 2 * channels]
            cross_ref[1 - low_first, b, p] = half[:, 2 * channels :]


def correlate(masks, own, low, high, frames, windows):
    sources, rows, channels = own[0].shape
    span = 2 * frames
    bins = rows // span
    in_spec = pl.BlockSpec((sources, BINS * span, channels), lambda i, masks: (0, i, 0))
    return pl.pallas_call(
        functools.partial(correlate_kernel, frames, windows),
        grid_spec=pltpu.PrefetchScalarGridSpec(
            num_scalar_prefetch=1,
            grid=(bins // BINS,),
            in_specs=[in_spec] * (3 * PARTS),
            out_specs=[
                pl.BlockSpec((2, BINS, 2, channels, channels), lambda i, masks: (0, i, 0, 0, 0)),
                pl.BlockSpec((BINS, 2, channels, channels), lambda i, masks: (i, 0, 0, 0)),
            ],
        ),
        out_shape=[
            jax.ShapeDtypeStruct((2, bins, 2, channels, channels), jnp.float32),
            jax.ShapeDtypeStruct((bins, 2, channels, channels), jnp.float32),
        ],
        compiler_params=pltpu.CompilerParams(vmem_limit_bytes=40 * 2**20),
    )(masks, *own, *low, *high)


def pair_exchange(index, pieces):
    blocks = lax.axis_size("chan")

    def branch(low, high, pieces):
        half = blocks // 2
        if not (low & half and high & half):
            return tuple([moved(piece, mask) for piece in pieces] for mask in (low, high))
        lead = low if low.bit_count() <= high.bit_count() else high
        leading, trailing = [], []
        for piece in pieces:
            if leading:
                piece, leading[-1] = lax.optimization_barrier((piece, leading[-1]))
            leading.append(moved(piece, lead))
            trailing.append(moved(leading[-1], low ^ high))
        return (leading, trailing) if lead == low else (trailing, leading)

    pairs = [(a, b) for a in range(1, blocks) for b in range(a + 1, blocks)]
    return lax.switch(index, [functools.partial(branch, a, b) for a, b in pairs], pieces)


def mask_exchange(mask, pieces):
    blocks = lax.axis_size("chan")
    branches = [
        lambda pieces, m=m: [moved(piece, m) for piece in pieces] for m in range(1, blocks)
    ]
    return lax.switch(mask - 1, branches, pieces)


def body(traces, kept_bins, round_masks):
    frames = traces.shape[1] // HOP
    ranks = lax.axis_size("freq")
    arrived, index = spectra_of(round_masks, traces, dft_table(kept_bins))
    step = ranks // PARTS
    own = tuple(arrived[i * step : (i + 1) * step] for i in range(PARTS))
    if lax.axis_size("chan") <= 8:
        low, high = pair_exchange(index[0], own)
    else:
        low = mask_exchange(jnp.minimum(round_masks[0], round_masks[1]), own)
        high = mask_exchange(jnp.maximum(round_masks[0], round_masks[1]), own)
    cross, auto = correlate(round_masks, own, low, high, frames, frames * ranks)
    return cross, auto


def solution(mesh):
    placed = (P("chan", "freq"), P(), P())
    return jax.shard_map(
        body,
        mesh=mesh,
        in_specs=placed,
        out_specs=(P(None, "freq", None, "chan", None), P("freq", None, "chan", None)),
        check_vma=False,
    )
```

```python
import functools
import math

import jax
import jax.numpy as jnp
from jax import lax
from jax.experimental import pallas as pl
from jax.experimental.pallas import tpu as pltpu
from jax.sharding import PartitionSpec as P

NS = 512
HOP = NS // 2
EPSILON = 1e-06
PARTS = 2
BINS = 4


def moved(piece, mask):
    route = [(i, i ^ mask) for i in range(lax.axis_size("chan"))]
    return lax.ppermute(piece, "chan", route)


def dft_table(kept_bins):
    sample_index = jnp.arange(NS, dtype=jnp.int32)
    phase_index = kept_bins[:, None] * sample_index[None, :] % NS
    angles = phase_index.astype(jnp.float32) * jnp.float32(2.0 * math.pi / NS)
    hann_taper = 0.5 - 0.5 * jnp.cos(
        sample_index.astype(jnp.float32) * jnp.float32(2.0 * math.pi / NS)
    )
    stacked = jnp.stack([hann_taper * jnp.cos(angles), -hann_taper * jnp.sin(angles)], axis=1)
    return stacked.reshape(kept_bins.shape[0] * 2, NS).astype(jnp.bfloat16)


def nt_dot(a, b):
    return lax.dot_general(a, b, (((1,), (1,)), ((), ())), preferred_element_type=jnp.float32)


def spectra_kernel(frames, ranks, *refs):
    masks_ref, traces_ref, transform_ref, arrived_ref, index_ref = refs[:5]
    rows, sends, following_ref, send_sem, recv_sem, own_sem, edge_sem = refs[5:]
    me = lax.axis_index("freq")
    peers = [lax.rem(me + d, ranks) for d in range(1, ranks)]
    barrier = pltpu.get_barrier_semaphore()
    for peer in peers:
        pl.semaphore_signal(
            barrier, inc=1, device_id={"freq": peer}, device_id_type=pl.DeviceIdType.MESH
        )
    low = jnp.minimum(masks_ref[0], masks_ref[1])
    high = jnp.maximum(masks_ref[0], masks_ref[1])
    before = (low - 1) * (lax.axis_size("chan") - 1) - lax.div(low * (low - 1), 2)
    index_ref[0] = before + high - low - 1
    edge = pltpu.make_async_remote_copy(
        src_ref=traces_ref.at[:, pl.ds(0, HOP)],
        dst_ref=following_ref,
        send_sem=edge_sem.at[0],
        recv_sem=edge_sem.at[1],
        device_id={"freq": lax.rem(me + ranks - 1, ranks)},
        device_id_type=pl.DeviceIdType.MESH,
    )
    count = transform_ref.shape[0]
    for w in range(frames - 1):
        if w == frames // 2:
            pl.semaphore_wait(barrier, ranks - 1)
            edge.start()
        rows[pl.ds(w, count, stride=frames), :] = nt_dot(
            transform_ref[...], traces_ref[:, w * HOP : w * HOP + NS]
        )
    last = nt_dot(transform_ref[:, :HOP], traces_ref[:, (frames - 1) * HOP :])
    edge.wait()
    beyond = nt_dot(transform_ref[:, HOP:], following_ref[...])
    last = last + jnp.where(me < ranks - 1, beyond, 0.0)
    rows[pl.ds(frames - 1, count, stride=frames), :] = last
    length = sends.shape[1]
    for r in range(ranks):
        sends[r] = rows[r * length : (r + 1) * length].astype(jnp.bfloat16)
    copies = [
        pltpu.make_async_remote_copy(
            src_ref=sends.at[peer],
            dst_ref=arrived_ref.at[me],
            send_sem=send_sem.at[i],
            recv_sem=recv_sem.at[i],
            device_id={"freq": peer},
            device_id_type=pl.DeviceIdType.MESH,
        )
        for i, peer in enumerate(peers)
    ]
    copies.append(pltpu.make_async_copy(sends.at[me], arrived_ref.at[me], own_sem))
    for copy in copies:
        copy.start()
    for copy in copies:
        copy.wait()


def spectra_of(masks, traces, transform):
    channels, samples = traces.shape
    frames = samples // HOP
    ranks = lax.axis_size("freq")
    total = transform.shape[0] * frames
    shape = (ranks, total // ranks, channels)
    return pl.pallas_call(
        functools.partial(spectra_kernel, frames, ranks),
        out_shape=[
            jax.ShapeDtypeStruct(shape, jnp.bfloat16),
            jax.ShapeDtypeStruct((1,), jnp.int32),
        ],
        in_specs=[
            pl.BlockSpec(memory_space=pltpu.SMEM),
            pl.BlockSpec(memory_space=pltpu.VMEM),
            pl.BlockSpec(memory_space=pltpu.VMEM),
        ],
        out_specs=[
            pl.BlockSpec(memory_space=pl.ANY),
            pl.BlockSpec(memory_space=pltpu.SMEM),
        ],
        scratch_shapes=[
            pltpu.VMEM((total, channels), jnp.float32),
            pltpu.VMEM(shape, jnp.bfloat16),
            pltpu.VMEM((channels, HOP), jnp.bfloat16),
            pltpu.SemaphoreType.DMA((ranks - 1,)),
            pltpu.SemaphoreType.DMA((ranks - 1,)),
            pltpu.SemaphoreType.DMA,
            pltpu.SemaphoreType.DMA((2,)),
        ],
        compiler_params=pltpu.CompilerParams(
            collective_id=0, has_side_effects=True, vmem_limit_bytes=32 * 2**20
        ),
    )(masks, traces, transform)


def correlate_kernel(frames, windows, masks_ref, *refs):
    *refs, out_ref = refs
    span = 2 * frames
    scale = 1.0 / math.sqrt(windows)
    low_first = jnp.where(masks_ref[0] > masks_ref[1], 1, 0)
    blocks = [
        [ref[s].astype(jnp.float32) for ref in refs[at : at + PARTS] for s in range(ref.shape[0])]
        for at in range(0, len(refs), PARTS)
    ]
    row = lax.broadcasted_iota(jnp.int32, (span, 1), 0)
    sign = jnp.where(row < frames, 1.0, -1.0).astype(jnp.float32)
    for b in range(BINS):
        whitened = []
        for block in blocks:
            values = [part[b * span : (b + 1) * span] for part in block]
            power = sum(jnp.sum(v * v, axis=0, keepdims=True) for v in values) / windows
            gain = lax.rsqrt(power + EPSILON)
            whitened.append([v * gain for v in values])
        left = jnp.concatenate(
            [
                jnp.concatenate([v, pltpu.roll(v, frames, 0) * sign], axis=1)
                for v in whitened[0]
            ],
            axis=0,
        ).astype(jnp.bfloat16)
        right = jnp.concatenate(
            [jnp.concatenate(columns, axis=1) for columns in zip(*(whitened[1:] or whitened))], axis=0
        ).astype(jnp.bfloat16)
        product = scale * lax.dot_general(
            left, right, (((0,), (0,)), ((), ())), preferred_element_type=jnp.float32
        )
        channels = product.shape[0] // 2
        for p in range(2):
            half = product[p * channels : (p + 1) * channels]
            if len(whitened) == 1:
                out_ref[b, p] = half
            else:
                out_ref[low_first, b, p] = half[:, :channels]
                out_ref[1 - low_first, b, p] = half[:, channels:]


def correlate(masks, blocks, frames, windows):
    sources, rows, channels = blocks[0].shape
    lead = () if len(blocks) == PARTS else (2,)
    home = (0,) * len(lead)
    span = 2 * frames
    bins = rows // span
    in_spec = pl.BlockSpec((sources, BINS * span, channels), lambda i, masks: (0, i, 0))
    return pl.pallas_call(
        functools.partial(correlate_kernel, frames, windows),
        grid_spec=pltpu.PrefetchScalarGridSpec(
            num_scalar_prefetch=1,
            grid=(bins // BINS,),
            in_specs=[in_spec] * len(blocks),
            out_specs=pl.BlockSpec(
                (*lead, BINS, 2, channels, channels), lambda i, masks: (*home, i, 0, 0, 0)
            ),
        ),
        out_shape=jax.ShapeDtypeStruct((*lead, bins, 2, channels, channels), jnp.float32),
        cost_estimate=pl.CostEstimate(
            flops=0, bytes_accessed=16 * bins * channels * channels, transcendentals=0
        ),
        compiler_params=pltpu.CompilerParams(vmem_limit_bytes=40 * 2**20),
    )(masks, *blocks)


def pair_exchange(index, masks, frames, windows, pieces):
    blocks = lax.axis_size("chan")

    def branch(low, high, pieces):
        half = blocks // 2
        auto = correlate(masks, pieces, frames, windows)
        if not (low & half and high & half):
            far = [[moved(piece, mask) for piece in pieces] for mask in (low, high)]
            return (*far, auto)
        lead = low if low.bit_count() <= high.bit_count() else high
        leading, trailing = [], []
        for piece in pieces:
            if leading:
                piece, leading[-1] = lax.optimization_barrier((piece, leading[-1]))
            leading.append(moved(piece, lead))
            trailing.append(moved(leading[-1], low ^ high))
        far = (leading, trailing) if lead == low else (trailing, leading)
        return (*far, auto)

    pairs = [(a, b) for a in range(1, blocks) for b in range(a + 1, blocks)]
    return lax.switch(index, [functools.partial(branch, a, b) for a, b in pairs], pieces)


def mask_exchange(mask, pieces):
    blocks = lax.axis_size("chan")
    branches = [
        lambda pieces, m=m: [moved(piece, m) for piece in pieces] for m in range(1, blocks)
    ]
    return lax.switch(mask - 1, branches, pieces)


def body(traces, kept_bins, round_masks):
    frames = traces.shape[1] // HOP
    ranks = lax.axis_size("freq")
    arrived, index = spectra_of(round_masks, traces, dft_table(kept_bins))
    step = ranks // PARTS
    own = tuple(arrived[i * step : (i + 1) * step] for i in range(PARTS))
    windows = frames * ranks
    if lax.axis_size("chan") <= 8:
        low, high, auto = pair_exchange(index[0], round_masks, frames, windows, own)
    else:
        low = mask_exchange(jnp.minimum(round_masks[0], round_masks[1]), own)
        high = mask_exchange(jnp.maximum(round_masks[0], round_masks[1]), own)
        auto = correlate(round_masks, own, frames, windows)
    cross = correlate(round_masks, (*own, *low, *high), frames, windows)
    return cross, auto


def solution(mesh):
    placed = (P("chan", "freq"), P(), P())
    return jax.shard_map(
        body,
        mesh=mesh,
        in_specs=placed,
        out_specs=(P(None, "freq", None, "chan", None), P("freq", None, "chan", None)),
        check_vma=False,
    )
```
